32 devices in a mesh: groups: 2 (over y), dp: 4 (over x, core), tensor: 4 (over z).
Axes of the slice: x: 2, y: 2, z: 4, core: 2. Of those that a mesh axis runs over, the one named last changes fastest.
Arguments:
- x_stream: bfloat16 [1024, 2048], P(('groups', 'dp'), 'tensor'), parts along dimension 0, may hold values from -24 to 24
- bc_stream: bfloat16 [1024, 1024], P(('groups', 'dp'), 'tensor'), parts along dimension 0, may hold values from -5 to 5
- gate_stream: bfloat16 [1024, 2048], P(('groups', 'dp'), 'tensor'), parts along dimension 0, may hold values from -5 to 5
- dt_stream: bfloat16 [1024, 32], P(('groups', 'dp'), 'tensor'), parts along dimension 0, may hold values from -4 to 4
- conv_x_state: bfloat16 [32, 3, 2048], P(('groups', 'dp'), None, 'tensor'), parts along dimension 0, may hold values from -5 to 5
- conv_bc_state: bfloat16 [32, 3, 1024], P(('groups', 'dp'), None, 'tensor'), parts along dimension 0, may hold values from -5 to 5
- ssm_state: bfloat16 [32, 32, 64, 256], P(('groups', 'dp'), 'tensor'), parts along dimension 0, may hold values from -5 to 5
- conv_x_weight: bfloat16 [4, 2048], P(None, 'tensor'), may hold values from -3 to 3
- conv_bc_weight: bfloat16 [4, 1024], P(None, 'tensor'), may hold values from -3 to 3
- dt_bias: float32 [32], P('tensor'), may hold values from -3 to 0
- decay_rate: float32 [32], P('tensor'), may hold values from 0.01 to 0.5
- skip_gain: float32 [32], P('tensor'), may hold values from 0.5 to 2
- norm_gain: float32 [2048], P('tensor'), may hold values from 0.25 to 1.75
- parents: int32 [32, 32], P(('groups', 'dp')), parts along dimension 0, may hold values from -1 to 30, as said below
- accepted: int32 [32], P(('groups', 'dp')), parts along dimension 0, may hold values from 0 to 31
- destination: int32 [32], P('groups'), parts along dimension 0, may hold values from -1 to 3, as said below
Outputs:
- y_out: bfloat16 [1024, 2048], P(('groups', 'dp'), 'tensor'), parts along dimension 0
- new_ssm_state: bfloat16 [48, 32, 64, 256], P(('groups', 'dp'), 'tensor'), parts along dimension 0
- new_conv_x: bfloat16 [48, 3, 2048], P(('groups', 'dp'), None, 'tensor'), parts along dimension 0
- new_conv_bc: bfloat16 [48, 3, 1024], P(('groups', 'dp'), None, 'tensor'), parts along dimension 0
The draws below stay inside these ranges and needn't reach their ends.
There are 2 independent parts, one for each index of `groups`. The reference program is written for one: setup_inputs(seed, part) draws one part's arguments, and reference() takes and returns one part's arrays. A program takes and returns all parts, laid end to end along the dimension named above; an argument that names none is the same for every part. Nothing has to cross between parts.
Inputs may be any that keep to these rules, and one draw needn't show every extreme that they name: `parents`: node 0 is the root with parent -1; every other node's parent is an earlier node. Exactly 2 of the 4 requests of each data index have a destination other than -1; no data index is the destination of more than 4 requests, and some data index is the destination of exactly 4.
All inputs are finite; a program needn't handle non-finite values.
Results may differ from the reference program's by a relative error of at most 0.006.
Values may be sent and summed in bfloat16 or wider, within the bound.
A program may use at most 64 MiB of HBM per device.

```python
import math
import jax
import jax.numpy as jnp
from jax import lax

P_SIZE = 64
N = 256
HG = 16
NODES = 32
REQ_DEV = 4
MOVE = 2
KEEP = 6
NG = 2
HEADS = 32
REQS = 16
TOKENS = 512
N_DP = 4


def draw_x_stream(key, part):
    key = jax.random.fold_in(key, 11)
    key_base, key_head, key_token = jax.random.split(key, 3)
    base = jnp.clip(jax.random.normal(key_base, (TOKENS, HEADS * P_SIZE), jnp.float32), -4.0, 4.0)
    head_scale = jnp.exp(jax.random.uniform(key_head, (HEADS,), jnp.float32, jnp.log(0.3), jnp.log(3.0)))
    token_scale = jnp.exp(jax.random.uniform(key_token, (TOKENS, 1), jnp.float32, jnp.log(0.5), jnp.log(2.0)))
    scaled = base * token_scale * jnp.repeat(head_scale, P_SIZE)[None, :]
    return scaled.astype(jnp.bfloat16)


def draw_parents(key, part):
    key = jax.random.fold_in(key, 22)
    back = jax.random.randint(key, (REQS, NODES), 1, 4)
    node_ids = jnp.arange(NODES, dtype=jnp.int32)[None, :]
    parent_ids = jnp.maximum(node_ids - back, 0)
    parent_ids = parent_ids.at[:, 0].set(-1)
    parent_ids = parent_ids.at[:, NODES - 1].set(NODES - 2)
    return parent_ids.astype(jnp.int32)


def draw_destination(key, part):
    key = jax.random.fold_in(key, 33)
    key_perm, key_labels, key_rank = jax.random.split(key, 3)
    order = jax.random.permutation(key_perm, N_DP)
    pattern = jnp.tile(jnp.array([2 * MOVE, MOVE, 0, MOVE], dtype=jnp.int32), N_DP // 4)
    counts = jnp.zeros((N_DP,), jnp.int32).at[order].set(pattern)
    last_empty = counts[N_DP - 1] == 0
    swapped = counts.at[order[1]].set(0).at[N_DP - 1].set(MOVE)
    counts = jnp.where(last_empty, swapped, counts)
    labels = jnp.repeat(jnp.arange(N_DP, dtype=jnp.int32), counts, total_repeat_length=N_DP * MOVE)
    labels = jax.random.permutation(key_labels, labels)
    scores = jax.random.randint(key_rank, (N_DP, REQ_DEV), 0, 1 << 20) * REQ_DEV + jnp.arange(REQ_DEV, dtype=jnp.int32)[None, :]
    ranks = jnp.argsort(jnp.argsort(scores, axis=1, stable=True), axis=1, stable=True).astype(jnp.int32)
    label_index = jnp.arange(N_DP, dtype=jnp.int32)[:, None] * MOVE + jnp.minimum(ranks, MOVE - 1)
    chosen = jnp.where(ranks < MOVE, labels[label_index], -1)
    return chosen.reshape(REQS).astype(jnp.int32)


def with_ends(entries, rng, smallest, largest):
    index_at = [jax.random.randint(jax.random.fold_in(rng, axis), (), 0, length) for axis, length in enumerate(entries.shape)]
    longest = entries.shape.index(max(entries.shape))
    beside = index_at[:longest] + [(index_at[longest] + 1) % entries.shape[longest]] + index_at[longest + 1:]
    return entries.at[tuple(index_at)].set(smallest).at[tuple(beside)].set(largest)


def shard_levels(rng, dims, pieces, least, top_value):
    def one(dim, parts):
        steps = jax.random.uniform(jax.random.fold_in(jax.random.fold_in(rng, 6), dim), (parts,), jnp.float32, least / len(pieces), top_value / len(pieces))
        return jnp.repeat(jnp.exp(steps), dims[dim] // parts).reshape((-1,) + (1,) * (len(dims) - dim - 1))

    loudness = one(*pieces[0])
    for cut in pieces[1:]:
        loudness = loudness * one(*cut)
    return loudness


def normal_values(stream_key, extent, width, most, cuts=(), kind=jnp.bfloat16):
    values = width * jax.random.normal(stream_key, extent, jnp.float32)
    if cuts:
        values = values * shard_levels(stream_key, extent, cuts, -0.22, 0.18)
    return jnp.clip(values, -most, most).astype(kind)


def setup_inputs(seed: int = 0, part: int = 0) -> dict:
    splits = jax.random.split(jax.random.key(seed), 17)
    part_splits = jax.random.split(jax.random.fold_in(splits[16], part), 17)
    return {
        "x_stream": draw_x_stream(jax.random.fold_in(jax.random.fold_in(splits[16], part), 71), part),
        "bc_stream": normal_values(part_splits[1], (TOKENS, 2 * NG * N), 1.0, 5.0, ((0, 4), (1, 4))),
        "gate_stream": normal_values(part_splits[2], (TOKENS, HEADS * P_SIZE), 1.0, 5.0, ((0, 4), (1, 4))),
        "dt_stream": normal_values(part_splits[3], (TOKENS, HEADS), 1.0, 4.0, ((0, 4), (1, 4))),
        "conv_x_state": normal_values(part_splits[4], (REQS, 3, HEADS * P_SIZE), 1.0, 5.0, ((0, 4), (2, 4))),
        "conv_bc_state": normal_values(part_splits[5], (REQS, 3, 2 * NG * N), 1.0, 5.0, ((0, 4), (2, 4))),
        "ssm_state": normal_values(part_splits[6], (REQS, HEADS, P_SIZE, N), 1.0, 5.0, ((0, 4), (1, 4))),
        "conv_x_weight": normal_values(splits[7], (4, HEADS * P_SIZE), 4 ** -0.5, 3.0, ((1, 4),)),
        "conv_bc_weight": normal_values(splits[8], (4, 2 * NG * N), 4 ** -0.5, 3.0, ((1, 4),)),
        "dt_bias": jnp.clip(-3.0 + 3.0 * jax.random.uniform(splits[9], (HEADS,), jnp.float32) ** shard_levels(splits[9], (HEADS,), ((0, 4),), -0.2, 0.2), -3.0, 0.0),
        "decay_rate": jnp.clip(jnp.exp(math.log(0.5) - 3.912023 * jax.random.uniform(splits[10], (HEADS,), jnp.float32) ** shard_levels(splits[10], (HEADS,), ((0, 4),), -0.2, 0.2)), 0.01, 0.5),
        "skip_gain": jnp.clip(0.5 + 1.5 * jax.random.uniform(splits[11], (HEADS,), jnp.float32) ** shard_levels(splits[11], (HEADS,), ((0, 4),), -0.2, 0.2), 0.5, 2.0),
        "norm_gain": jnp.clip(1.0 + 0.15 * jax.random.normal(splits[12], (HEADS * P_SIZE,), jnp.float32), 0.25, 1.75),
        "parents": draw_parents(jax.random.fold_in(jax.random.fold_in(splits[16], part), 71), part),
        "accepted": with_ends(jax.random.randint(part_splits[14], (REQS,), 0, NODES), jax.random.fold_in(part_splits[14], 1), 0, NODES - 1).astype(jnp.int32),
        "destination": draw_destination(jax.random.fold_in(jax.random.fold_in(splits[16], part), 71), part),
    }


def ancestor_tap(values, history, chain, depths, k):
    here = chain[k]
    lag_row = jnp.clip(3 - k + depths, 0, 2)
    return jnp.where((here >= 0)[:, None], values[jnp.maximum(here, 0)], history[lag_row])

def reference(x_stream, bc_stream, gate_stream, dt_stream, conv_x_state, conv_bc_state, ssm_state, conv_x_weight, conv_bc_weight, dt_bias, decay_rate, skip_gain, norm_gain, parents, accepted, destination):
    highest = lax.Precision.HIGHEST
    x_taps_weight = conv_x_weight.astype(jnp.float32)
    bc_taps_weight = conv_bc_weight.astype(jnp.float32)

    def single(item):
        x_rows, bc_rows, gate_rows, dt_rows, x_history, bc_history, prior_state, parent_row, accept = item
        node_ids = jnp.arange(NODES, dtype=jnp.int32)
        links = [node_ids]
        current = node_ids
        for k in range(NODES - 1):
            current = jnp.where(current >= 0, parent_row[jnp.maximum(current, 0)], -1)
            links.append(current)
        chain = jnp.stack(links)
        on_path = jnp.any(chain[:, :, None] == node_ids[None, None, :], axis=0)
        depths = lax.optimization_barrier(jnp.sum(on_path.astype(jnp.int32), axis=1)) - 1

        def convolve(values, history, weight):
            summed = jnp.zeros(values.shape, jnp.float32)
            for k in range(4):
                summed = summed + weight[k] * ancestor_tap(values, history, chain, depths, k).astype(jnp.float32)
            return jax.nn.silu(summed).astype(jnp.bfloat16)
        x_act = convolve(x_rows, x_history, x_taps_weight)
        bc_act = convolve(bc_rows, bc_history, bc_taps_weight)
        step_size = jax.nn.softplus(dt_rows.astype(jnp.float32) + dt_bias)
        step_decay = -decay_rate * step_size
        path_float = on_path.astype(jnp.float32)
        logdecay = jnp.dot(path_float, step_decay, precision=highest)
        paired = bc_act.reshape(NODES, NG, 2, N)
        b_nodes = paired[:, :, 0, :]
        c_nodes = paired[:, :, 1, :]
        inner = jnp.einsum('ign,jgn->gij', c_nodes.astype(jnp.float32), b_nodes.astype(jnp.float32), precision=highest)
        inner_heads = jnp.repeat(inner, HG, axis=0)
        inside = on_path[:, :, None]
        spread = jnp.where(inside, logdecay[:, None, :] - logdecay[None, :, :], -1e+30)
        decay = jnp.where(inside, jnp.exp(spread), 0.0) * step_size[None, :, :]
        weights = (inner_heads * jnp.transpose(decay, (2, 0, 1))).astype(jnp.bfloat16)
        x_heads = x_act.reshape(NODES, HEADS, P_SIZE).astype(jnp.float32)
        tree_part = jnp.einsum('hij,jhp->ihp', weights.astype(jnp.float32), x_heads, precision=highest)
        c_heads = jnp.repeat(c_nodes, HG, axis=1).astype(jnp.float32)
        held = jnp.einsum('ihn,hpn->ihp', c_heads, prior_state.astype(jnp.float32), precision=highest)
        held = held * jnp.exp(logdecay)[:, :, None]
        mixed = tree_part + held + skip_gain[None, :, None] * x_heads
        gated = mixed * jax.nn.silu(gate_rows.reshape(NODES, HEADS, P_SIZE).astype(jnp.float32))
        grouped = gated.reshape(NODES, NG, HG * P_SIZE)
        mean_square = lax.optimization_barrier(jnp.mean(grouped * grouped, axis=-1, keepdims=True))
        normed = (grouped * lax.rsqrt(mean_square + 1e-05)).reshape(NODES, HEADS * P_SIZE)
        y_rows = (normed * norm_gain[None, :]).astype(jnp.bfloat16)
        accept_row = on_path[accept]
        accept_log = logdecay[accept]
        reach = jnp.where(accept_row[:, None], accept_log[None, :] - logdecay, -1e+30)
        coef = (jnp.where(accept_row[:, None], jnp.exp(reach), 0.0) * step_size).astype(jnp.bfloat16)
        scaled_x = coef.astype(jnp.float32)[:, :, None] * x_heads
        b_heads = jnp.repeat(b_nodes, HG, axis=1).astype(jnp.float32)
        fresh = jnp.exp(accept_log)[:, None, None] * prior_state.astype(jnp.float32)
        fresh = fresh + jnp.einsum('jhp,jhn->hpn', scaled_x, b_heads, precision=highest)
        fresh = fresh.astype(jnp.bfloat16)
        fresh_x = jnp.stack([ancestor_tap(x_rows, x_history, chain, depths, 2 - t)[accept] for t in range(3)])
        fresh_bc = jnp.stack([ancestor_tap(bc_rows, bc_history, chain, depths, 2 - t)[accept] for t in range(3)])
        return (y_rows, fresh, fresh_x, fresh_bc)
    items = (x_stream.reshape(REQS, NODES, HEADS * P_SIZE), bc_stream.reshape(REQS, NODES, 2 * NG * N), gate_stream.reshape(REQS, NODES, HEADS * P_SIZE), dt_stream.reshape(REQS, NODES, HEADS), conv_x_state, conv_bc_state, ssm_state, parents, accepted)
    y_rows, fresh, fresh_x, fresh_bc = lax.map(single, items)
    y_out = y_rows.reshape(TOKENS, HEADS * P_SIZE)
    request_ids = jnp.arange(REQS, dtype=jnp.int32)
    home = request_ids // REQ_DEV
    staying = destination < 0
    stay_rank = (jnp.cumsum(staying.astype(jnp.int32).reshape(N_DP, REQ_DEV), axis=1) - 1).reshape(REQS)
    target = jnp.where(staying, home, destination)
    arrive_hot = ((target[:, None] == jnp.arange(N_DP, dtype=jnp.int32)[None, :]) & (~staying)[:, None]).astype(jnp.int32)
    move_rank = lax.optimization_barrier(jnp.sum((jnp.cumsum(arrive_hot, axis=0) - 1) * arrive_hot, axis=1))
    slot_index = jnp.where(staying, stay_rank, REQ_DEV - MOVE + move_rank)
    flat_slot = (target * KEEP + slot_index).astype(jnp.int32)
    new_ssm_state = jnp.zeros((N_DP * KEEP, HEADS, P_SIZE, N), jnp.bfloat16).at[flat_slot].set(fresh)
    new_conv_x = jnp.zeros((N_DP * KEEP, 3, HEADS * P_SIZE), jnp.bfloat16).at[flat_slot].set(fresh_x)
    new_conv_bc = jnp.zeros((N_DP * KEEP, 3, 2 * NG * N), jnp.bfloat16).at[flat_slot].set(fresh_bc)
    return (y_out, new_ssm_state, new_conv_x, new_conv_bc)
```

```python
import functools

import jax
import jax.numpy as jnp
from jax import lax
from jax.experimental import pallas as pl
from jax.experimental.pallas import tpu as pltpu
from jax.sharding import PartitionSpec as P

P_SIZE = 64
N = 256
NODES = 32
MOVE = 2
IN_CAP = 4
KEEP = 6
CHUNKS = 4
MESH = pl.DeviceIdType.MESH
F32 = jnp.float32
BF16 = jnp.bfloat16


def mm(a, b):
    return jnp.dot(a.astype(BF16), b.astype(BF16), preferred_element_type=F32)


def mm_exact(a, b):
    return jnp.dot(a, b, preferred_element_type=F32, precision=lax.Precision.HIGHEST)


def iota(shape, dim):
    return lax.broadcasted_iota(jnp.int32, shape, dim)


def silu(v):
    return v / (1.0 + jnp.exp(-v))


def kernel(
    n_dp,
    x_ref,
    bc_ref,
    gate_ref,
    dt_ref,
    hx_ref,
    hbc_ref,
    ssm_ref,
    wx_ref,
    wbc_ref,
    bias_ref,
    rate_ref,
    skip_ref,
    gain_ref,
    par_ref,
    acc_ref,
    dst_ref,
    y_ref,
    new_ref,
    ncx_ref,
    ncbc_ref,
    hist_x,
    hist_bc,
    own_bc,
    other_bc,
    sq_own,
    sq_other,
    taps,
    *rest,
):
    bufs = rest[:CHUNKS]
    t_send, t_recv, x_send, x_recv, p_send, p_recv = rest[CHUNKS:]
    chips = n_dp // 2
    me = lax.axis_index("dp")
    chip = me // 2
    core = me % 2
    tensor = lax.axis_index("tensor")
    parity = tensor % 2
    mate = tensor + 1 - 2 * parity
    twin = me + 1 - 2 * core

    def ahead(j):
        return 2 * ((chip + j) % chips) + core

    def behind(j, which):
        return 2 * ((chip + chips - j) % chips) + which

    barrier = pltpu.get_barrier_semaphore()
    pl.semaphore_signal(barrier, inc=1, device_id={"tensor": mate}, device_id_type=MESH)
    pl.semaphore_signal(barrier, inc=1, device_id={"dp": twin}, device_id_type=MESH)
    for j in range(1, chips):
        pl.semaphore_signal(barrier, inc=1, device_id={"dp": ahead(j)}, device_id_type=MESH)

    requests = par_ref.shape[0]
    rows = x_ref.shape[0]
    heads = dt_ref.shape[1]
    width = x_ref.shape[1]

    stay = [jnp.int32(0)] * (requests - MOVE)
    move = [jnp.int32(0)] * MOVE
    stay_count = jnp.int32(0)
    move_count = jnp.int32(0)
    for q in range(requests):
        staying = dst_ref[me * requests + q] < 0
        for k in range(requests - MOVE):
            stay[k] = jnp.where(staying & (stay_count == k), q, stay[k])
        for k in range(MOVE):
            move[k] = jnp.where(jnp.logical_not(staying) & (move_count == k), q, move[k])
        stay_count = stay_count + jnp.where(staying, 1, 0)
        move_count = move_count + jnp.where(staying, 0, 1)
    source = [jnp.int32(-1)] * IN_CAP
    arrived = jnp.int32(0)
    for d in range(n_dp):
        rank = jnp.int32(0)
        for q in range(requests):
            to = dst_ref[d * requests + q]
            mine = to == me
            for k in range(IN_CAP):
                source[k] = jnp.where(mine & (arrived == k), d * MOVE + rank, source[k])
            arrived = arrived + jnp.where(mine, 1, 0)
            rank = rank + jnp.where(to >= 0, 1, 0)

    row = iota((rows, rows), 0)
    col = iota((rows, rows), 1)
    tile = (iota((NODES, rows), 1) % NODES == iota((NODES, rows), 0)).astype(F32)
    tiled = mm(par_ref[...].astype(F32), tile)
    owner = iota((requests, rows), 0)
    flat = jnp.where(tiled < -0.5, -1.0, tiled + (NODES * owner).astype(F32))
    flat = jnp.sum(
        jnp.where(iota((requests, rows), 1) // NODES == owner, flat, 0.0), axis=0, keepdims=True
    )
    hop_t = jnp.where(row.astype(F32) == flat, 1.0, 0.0)
    eye = jnp.where(row == col, 1.0, 0.0)
    hop1 = hop_t.T
    hop2 = mm(hop1, hop1)
    hop3 = mm(hop2, hop1)
    hop4 = mm(hop2, hop2)
    hop8 = mm(hop4, hop4)
    hop16 = mm(hop8, hop8)
    path = eye + hop1
    path = path + mm(hop2, path)
    path = path + mm(hop4, path)
    path = path + mm(hop8, path)
    path = path + mm(hop16, path)
    depth = jnp.sum(path, axis=1, keepdims=True) - 1.0
    hops = [eye, hop1, hop2, hop3]
    hist_rows = 8 * requests
    hist_row = iota((rows, hist_rows), 1)
    hist_mine = (hist_row // 8 == iota((rows, hist_rows), 0) // NODES) & (hist_row % 8 < 3)
    lags = [
        jnp.where(hist_mine & ((hist_row % 8).astype(F32) == 3.0 - k + depth), 1.0, 0.0)
        for k in range(4)
    ]

    hist_x[...] = jnp.zeros(hist_x.shape, F32)
    hist_bc[...] = jnp.zeros(hist_bc.shape, F32)
    for r in range(requests):
        hist_x[8 * r : 8 * r + 3, :] = hx_ref[r].astype(F32)
        hist_bc[8 * r : 8 * r + 3, :] = hbc_ref[r].astype(F32)

    def convolve(values, history, w_ref):
        summed = w_ref[0:1, :].astype(F32) * values.astype(F32)
        for k in range(1, 4):
            tap = mm(hops[k], values) + mm(lags[k], history)
            summed = summed + w_ref[k : k + 1, :].astype(F32) * tap
        return silu(summed).astype(BF16)

    own_bc[...] = convolve(bc_ref[...], hist_bc[...], wbc_ref)

    pl.semaphore_wait(barrier, 1 + chips)
    bc_copy = pltpu.make_async_remote_copy(
        src_ref=own_bc,
        dst_ref=other_bc,
        send_sem=t_send.at[0],
        recv_sem=t_recv.at[0],
        device_id={"tensor": mate},
        device_id_type=MESH,
    )
    bc_copy.start()

    x_act = convolve(x_ref[...], hist_x[...], wx_ref)

    raw = dt_ref[...].astype(F32) + bias_ref[...]
    step = jnp.maximum(raw, 0.0) + jnp.log1p(jnp.exp(-jnp.abs(raw)))
    step_decay = -rate_ref[...] * step
    log = mm_exact(path, step_decay)

    target = jnp.zeros((rows, rows), jnp.int32)
    for r in range(requests):
        target = jnp.where(row // NODES == r, NODES * r + acc_ref[r], target)
    accept_hot = jnp.where(col == target, 1.0, 0.0)
    accept_log = mm_exact(accept_hot, log)
    accept_path = jnp.sum(accept_hot * path.T, axis=1, keepdims=True) > 0.5
    reach = jnp.where(accept_path, accept_log - log, -1e30)
    coef = (jnp.where(accept_path, jnp.exp(reach), 0.0) * step).astype(BF16).astype(F32)
    accept_exp = jnp.exp(accept_log)

    lane_low = iota((1, 2 * P_SIZE), 1) < P_SIZE

    def expand(v):
        return jnp.concatenate(
            [
                jnp.where(lane_low, v[:, 2 * q : 2 * q + 1], v[:, 2 * q + 1 : 2 * q + 2])
                for q in range(heads // 2)
            ],
            axis=1,
        )

    x_float = x_act.astype(F32)
    scaled_t = (expand(coef) * x_float).T.astype(BF16)

    def tap_rows():
        pick = iota((8 * requests, rows), 0)
        ids = stay + move
        wanted = jnp.zeros((8 * requests, rows), jnp.int32)
        for k in range(requests):
            wanted = jnp.where(pick // 8 == k, NODES * ids[k] + acc_ref[ids[k]], wanted)
        hot = jnp.where(iota((8 * requests, rows), 1) == wanted, 1.0, 0.0)
        turn = pick % 8
        node_part = jnp.where(
            turn == 2, hot, jnp.where(turn == 1, mm(hot, hops[1]), mm(hot, hops[2]))
        )
        turn = iota((8 * requests, hist_rows), 0) % 8
        lag_part = jnp.where(
            turn == 2, 0.0, jnp.where(turn == 1, mm(hot, lags[1]), mm(hot, lags[2]))
        )
        fx = mm(node_part, x_ref[...]) + mm(lag_part, hist_x[...])
        fbc = mm(node_part, bc_ref[...]) + mm(lag_part, hist_bc[...])
        return fx.astype(BF16), fbc.astype(BF16)

    fresh_x, fresh_bc = tap_rows()
    stays = requests - MOVE
    taps[me] = jnp.concatenate([fresh_x[8 * stays :], fresh_bc[8 * stays :]], axis=1)
    for k in range(stays):
        ncx_ref[k] = fresh_x[8 * k : 8 * k + 3]
        ncbc_ref[k] = fresh_bc[8 * k : 8 * k + 3]

    bc_copy.wait()
    own = own_bc[...]
    other = other_bc[...]
    even = (parity == 0).astype(F32)
    own_f = own.astype(F32)
    other_f = other.astype(F32)
    b_act = (even * own_f + (1.0 - even) * other_f).astype(BF16)
    c_act = (even * other_f + (1.0 - even) * own_f).astype(BF16)

    row_request = iota((rows, 1), 0) // NODES
    first_row = iota((rows, 1), 0)
    per = heads // CHUNKS
    depth_rows = per * P_SIZE

    def fresh_of(request):
        b_mine = jnp.where(row_request == request, b_act.astype(F32), 0.0).astype(BF16)
        scale = jnp.sum(
            jnp.where(first_row == NODES * request, accept_exp, 0.0), axis=0, keepdims=True
        )

        def chunk(c):
            update = mm(scaled_t[c * depth_rows : (c + 1) * depth_rows], b_mine)
            parts = []
            for h in range(per):
                head = c * per + h
                held = ssm_ref[request, head].astype(F32) * scale[:, head : head + 1]
                parts.append(held + update[h * P_SIZE : (h + 1) * P_SIZE])
            return jnp.concatenate(parts, axis=0).astype(BF16)

        return chunk

    def block_of(c, device):
        if c == CHUNKS:
            return taps.at[device]
        return bufs[c].at[pl.ds(device * MOVE, MOVE)]

    def across(c, j, device):
        return pltpu.make_async_remote_copy(
            src_ref=block_of(c, device),
            dst_ref=block_of(c, device),
            send_sem=x_send.at[c, j],
            recv_sem=x_recv.at[c, j],
            device_id={"dp": ahead(j)},
            device_id_type=MESH,
        )

    def beside(c, j, device):
        return pltpu.make_async_remote_copy(
            src_ref=block_of(c, device),
            dst_ref=block_of(c, device),
            send_sem=p_send.at[c, j],
            recv_sem=p_recv.at[c, j],
            device_id={"dp": twin},
            device_id_type=MESH,
        )

    def send(c):
        for j in range(1, chips):
            across(c, j, me).start()
        beside(c, 0, me).start()

    def relay(c):
        for j in range(1, chips):
            across(c, j, behind(j, core)).wait_recv()
            beside(c, j, behind(j, core)).start()

    def place(c):
        for j in range(chips):
            beside(c, j, behind(j, 1 - core)).wait_recv()
        for k in range(IN_CAP):
            index = jnp.maximum(source[k], 0)
            there = source[k] >= 0
            if c == CHUNKS:
                found = taps[index // MOVE].astype(F32)
                found = jnp.where(index % MOVE == 0, found[0:8], found[8:16])
                found = jnp.where(there, found, 0.0).astype(BF16)
                ncx_ref[stays + k] = found[0:3, :width]
                ncbc_ref[stays + k] = found[0:3, width:]
            else:
                found = jnp.where(there, bufs[c][index].astype(F32), 0.0).astype(BF16)
                new_ref[stays + k, c * per : (c + 1) * per] = found.reshape(per, P_SIZE, N)

    movers = [fresh_of(move[k]) for k in range(MOVE)]
    for c in range(CHUNKS):
        for k in range(MOVE):
            bufs[c][me * MOVE + k] = movers[k](c)
        send(c)
    send(CHUNKS)

    inner = lax.dot_general(
        c_act, b_act, (((1,), (1,)), ((), ())), preferred_element_type=F32
    )
    inside = path > 0.5
    inner = jnp.where(inside, inner, 0.0)
    log_t = log.T
    step_t = step.T
    log_exp = expand(jnp.exp(log))
    held = jnp.concatenate(
        [
            lax.dot_general(
                c_act[NODES * r : NODES * (r + 1)],
                ssm_ref[r].reshape(width, N),
                (((1,), (1,)), ((), ())),
                preferred_element_type=F32,
            )
            for r in range(requests)
        ],
        axis=0,
    )
    tree = []
    for q in range(heads // 2):
        pair = x_act[:, 2 * P_SIZE * q : 2 * P_SIZE * (q + 1)]
        both = []
        for h in (2 * q, 2 * q + 1):
            spread = jnp.where(inside, log[:, h : h + 1] - log_t[h : h + 1, :], -1e30)
            weight = inner * jnp.exp(spread) * step_t[h : h + 1, :]
            both.append(mm(weight, pair))
        tree.append(jnp.where(lane_low, both[0], both[1]))
    tree = jnp.concatenate(tree, axis=1)
    mixed = tree + held * log_exp + expand(skip_ref[...]) * x_float
    gated = mixed * silu(gate_ref[...].astype(F32))
    squares = jnp.sum(gated * gated, axis=1, keepdims=True)
    sq_own[...] = jnp.broadcast_to(
        jnp.sum(jnp.where(row == col, squares, 0.0), axis=0, keepdims=True), sq_own.shape
    )
    sq_copy = pltpu.make_async_remote_copy(
        src_ref=sq_own,
        dst_ref=sq_other,
        send_sem=t_send.at[1],
        recv_sem=t_recv.at[1],
        device_id={"tensor": mate},
        device_id_type=MESH,
    )
    sq_copy.start()

    relay(0)
    for k in range(stays):
        chunk = fresh_of(stay[k])
        for c in range(CHUNKS):
            new_ref[k, c * per : (c + 1) * per] = chunk(c).reshape(per, P_SIZE, N)

    sq_copy.wait()
    partner = jnp.sum(jnp.where(row == col, sq_other[0:1, :], 0.0), axis=1, keepdims=True)
    mean_square = (squares + partner) * (1.0 / (2 * heads * P_SIZE))
    y_ref[...] = (gated * lax.rsqrt(mean_square + 1e-05) * gain_ref[...]).astype(BF16)

    for c in range(1, CHUNKS + 1):
        relay(c)
        place(c - 1)
    place(CHUNKS)
    for c in range(CHUNKS + 1):
        for j in range(1, chips):
            across(c, j, me).wait_send()
        for j in range(chips):
            beside(c, j, behind(j, core)).wait_send()


def body(
    x_stream,
    bc_stream,
    gate_stream,
    dt_stream,
    conv_x_state,
    conv_bc_state,
    ssm_state,
    conv_x_weight,
    conv_bc_weight,
    dt_bias,
    decay_rate,
    skip_gain,
    norm_gain,
    parents,
    accepted,
    destination,
):
    n_dp = lax.axis_size("dp")
    chips = n_dp // 2
    rows, width = x_stream.shape
    bc_width = bc_stream.shape[1]
    requests = parents.shape[0]
    heads = dt_stream.shape[1]
    vmem = pl.BlockSpec(memory_space=pltpu.VMEM)
    smem = pl.BlockSpec(memory_space=pltpu.SMEM)
    copies = (CHUNKS + 1, chips)
    return pl.pallas_call(
        functools.partial(kernel, n_dp),
        out_shape=(
            jax.ShapeDtypeStruct((rows, width), BF16),
            jax.ShapeDtypeStruct((KEEP, heads, P_SIZE, N), BF16),
            jax.ShapeDtypeStruct((KEEP, 3, width), BF16),
            jax.ShapeDtypeStruct((KEEP, 3, bc_width), BF16),
        ),
        in_specs=[vmem] * 14 + [smem] * 2,
        out_specs=(vmem,) * 4,
        scratch_shapes=[
            pltpu.VMEM((8 * requests, width), F32),
            pltpu.VMEM((8 * requests, bc_width), F32),
            pltpu.VMEM((rows, bc_width), BF16),
            pltpu.VMEM((rows, bc_width), BF16),
            pltpu.VMEM((8, rows), F32),
            pltpu.VMEM((8, rows), F32),
            pltpu.VMEM((n_dp, 8 * MOVE, width + bc_width), BF16),
        ]
        + [
            pltpu.VMEM((n_dp * MOVE, heads // CHUNKS * P_SIZE, N), BF16) for _ in range(CHUNKS)
        ]
        + [pltpu.SemaphoreType.DMA((2,))] * 2
        + [pltpu.SemaphoreType.DMA(copies)] * 4,
        compiler_params=pltpu.CompilerParams(
            collective_id=0, has_side_effects=True, vmem_limit_bytes=40 << 20
        ),
        name="verify_and_migrate",
    )(
        x_stream,
        bc_stream,
        gate_stream,
        dt_stream,
        conv_x_state,
        conv_bc_state,
        ssm_state,
        conv_x_weight,
        conv_bc_weight,
        dt_bias.reshape(1, heads),
        decay_rate.reshape(1, heads),
        skip_gain.reshape(1, heads),
        norm_gain.reshape(1, width),
        parents,
        accepted,
        destination,
    )


def solution(mesh):
    placed = (
        P(("groups", "dp"), "tensor"),
        P(("groups", "dp"), "tensor"),
        P(("groups", "dp"), "tensor"),
        P(("groups", "dp"), "tensor"),
        P(("groups", "dp"), None, "tensor"),
        P(("groups", "dp"), None, "tensor"),
        P(("groups", "dp"), "tensor", None, None),
        P(None, "tensor"),
        P(None, "tensor"),
        P("tensor"),
        P("tensor"),
        P("tensor"),
        P("tensor"),
        P(("groups", "dp"), None),
        P(("groups", "dp")),
        P("groups"),
    )
    return jax.shard_map(
        body,
        mesh=mesh,
        in_specs=placed,
        out_specs=(
            P(("groups", "dp"), "tensor"),
            P(("groups", "dp"), "tensor", None, None),
            P(("groups", "dp"), None, "tensor"),
            P(("groups", "dp"), None, "tensor"),
        ),
        check_vma=False,
    )
```

```python
import functools

import jax
import jax.numpy as jnp
from jax import lax
from jax.experimental import pallas as pl
from jax.experimental.pallas import tpu as pltpu
from jax.sharding import PartitionSpec as P

P_SIZE = 64
N = 256
NODES = 32
MOVE = 2
IN_CAP = 4
KEEP = 6
CHUNKS = 8
RAW = 4
TAPS, AUX, SCALE = CHUNKS, CHUNKS + 1, CHUNKS + 2
MESSAGES = CHUNKS + 3
MESH = pl.DeviceIdType.MESH
F32 = jnp.float32
BF16 = jnp.bfloat16


def mm(a, b):
    return jnp.dot(a.astype(BF16), b.astype(BF16), preferred_element_type=F32)


def mm_exact(a, b):
    return jnp.dot(a, b, preferred_element_type=F32, precision=lax.Precision.HIGHEST)


def iota(shape, dim):
    return lax.broadcasted_iota(jnp.int32, shape, dim)


def silu(v):
    return v / (1.0 + jnp.exp(-v))


def kernel(n_dp, *refs):
    operands = refs[:16]
    y_ref, new_ref, ncx_ref, ncbc_ref = refs[16:20]
    held_refs = refs[20:36]
    hist_x, hist_bc, own_bc, other_bc, sq_own, sq_other, xs_rows, b_rows = refs[36:44]
    bufs = refs[44 : 44 + MESSAGES]
    in_sem, t_send, t_recv, x_send, x_recv, p_send, p_recv = refs[44 + MESSAGES :]
    (
        x_ref,
        bc_ref,
        gate_ref,
        dt_ref,
        hx_ref,
        hbc_ref,
        ssm_ref,
        wx_ref,
        wbc_ref,
        bias_ref,
        rate_ref,
        skip_ref,
        gain_ref,
        par_ref,
        acc_ref,
        dst_ref,
    ) = held_refs
    loads = [
        pltpu.make_async_copy(operands[i], held_refs[i], in_sem.at[i]) for i in range(16)
    ]
    names = ("x", "bc", "gate", "dt", "hx", "hbc", "ssm", "wx", "wbc")
    names += ("bias", "rate", "skip", "gain", "par", "acc", "dst")
    load = dict(zip(names, loads))
    chips = n_dp // 2
    me = lax.axis_index("dp")
    chip = me // 2
    core = me % 2
    tensor = lax.axis_index("tensor")
    parity = tensor % 2
    mate = tensor + 1 - 2 * parity
    twin = me + 1 - 2 * core

    def ahead(j):
        return 2 * ((chip + j) % chips) + core

    def behind(j, which):
        return 2 * ((chip + chips - j) % chips) + which

    barrier = pltpu.get_barrier_semaphore()
    pl.semaphore_signal(barrier, inc=1, device_id={"tensor": mate}, device_id_type=MESH)
    pl.semaphore_signal(barrier, inc=1, device_id={"dp": twin}, device_id_type=MESH)
    for j in range(1, chips):
        pl.semaphore_signal(barrier, inc=1, device_id={"dp": ahead(j)}, device_id_type=MESH)

    order = ("dst", "ssm", "par", "bc", "hbc", "wbc", "acc", "x", "hx", "wx")
    order += ("dt", "bias", "rate", "gate", "skip", "gain")
    for name in order:
        load[name].start()

    requests = par_ref.shape[0]
    rows = x_ref.shape[0]
    heads = dt_ref.shape[0]
    width = x_ref.shape[1]

    load["dst"].wait()
    stay = [jnp.int32(0)] * (requests - MOVE)
    move = [jnp.int32(0)] * MOVE
    stay_count = jnp.int32(0)
    move_count = jnp.int32(0)
    for q in range(requests):
        staying = dst_ref[me * requests + q] < 0
        for k in range(requests - MOVE):
            stay[k] = jnp.where(staying & (stay_count == k), q, stay[k])
        for k in range(MOVE):
            move[k] = jnp.where(jnp.logical_not(staying) & (move_count == k), q, move[k])
        stay_count = stay_count + jnp.where(staying, 1, 0)
        move_count = move_count + jnp.where(staying, 0, 1)
    stays = requests - MOVE
    per = heads // CHUNKS
    depth_rows = per * P_SIZE

    def block_of(c, device):
        if c in (TAPS, SCALE):
            return bufs[c].at[device]
        return bufs[c].at[pl.ds(device * MOVE, MOVE)]

    def across(c, j, device):
        return pltpu.make_async_remote_copy(
            src_ref=block_of(c, device),
            dst_ref=block_of(c, device),
            send_sem=x_send.at[c, j],
            recv_sem=x_recv.at[c, j],
            device_id={"dp": ahead(j)},
            device_id_type=MESH,
        )

    def beside(c, j, device):
        return pltpu.make_async_remote_copy(
            src_ref=block_of(c, device),
            dst_ref=block_of(c, device),
            send_sem=p_send.at[c, j],
            recv_sem=p_recv.at[c, j],
            device_id={"dp": twin},
            device_id_type=MESH,
        )

    def send(c):
        for j in range(1, chips):
            across(c, j, me).start()
        beside(c, 0, me).start()

    def relay(c):
        for j in range(1, chips):
            across(c, j, behind(j, core)).wait_recv()
            beside(c, j, behind(j, core)).start()

    load["ssm"].wait()
    for c in range(RAW):
        for k in range(MOVE):
            part = ssm_ref[move[k], c * per : (c + 1) * per]
            bufs[c][me * MOVE + k] = part.reshape(depth_rows, N)
    pl.semaphore_wait(barrier, 1 + chips)
    for c in range(RAW):
        send(c)

    load["par"].wait()
    row = iota((rows, rows), 0)
    col = iota((rows, rows), 1)
    tile = (iota((NODES, rows), 1) % NODES == iota((NODES, rows), 0)).astype(F32)
    tiled = mm(par_ref[...].astype(F32), tile)
    owner = iota((requests, rows), 0)
    flat = jnp.where(tiled < -0.5, -1.0, tiled + (NODES * owner).astype(F32))
    flat = jnp.sum(
        jnp.where(iota((requests, rows), 1) // NODES == owner, flat, 0.0), axis=0, keepdims=True
    )
    hop_t = jnp.where(row.astype(F32) == flat, 1.0, 0.0)
    eye = jnp.where(row == col, 1.0, 0.0)
    hop1 = hop_t.T
    hop2 = mm(hop1, hop1)
    hop3 = mm(hop2, hop1)
    hop4 = mm(hop2, hop2)
    hop8 = mm(hop4, hop4)
    hop16 = mm(hop8, hop8)
    path = eye + hop1
    path = path + mm(hop2, path)
    path = path + mm(hop4, path)
    path = path + mm(hop8, path)
    path = path + mm(hop16, path)
    depth = jnp.sum(path, axis=1, keepdims=True) - 1.0
    hops = [eye, hop1, hop2, hop3]
    hist_rows = 32
    hist_row = iota((rows, hist_rows), 1)
    hist_mine = (hist_row % 8 == iota((rows, hist_rows), 0) // NODES) & (hist_row < 24)
    lags = [
        jnp.where(hist_mine & ((hist_row // 8).astype(F32) == 3.0 - k + depth), 1.0, 0.0)
        for k in range(4)
    ]

    hist_x[...] = jnp.zeros(hist_x.shape, F32)
    hist_bc[...] = jnp.zeros(hist_bc.shape, F32)
    load["hbc"].wait()
    for t in range(3):
        hist_bc[8 * t : 8 * t + requests, :] = hbc_ref[t].astype(F32)

    def convolve(values, history, w_ref):
        summed = w_ref[0:1, :].astype(F32) * values.astype(F32)
        for k in range(1, 4):
            tap = mm(hops[k], values) + mm(lags[k], history)
            summed = summed + w_ref[k : k + 1, :].astype(F32) * tap
        return silu(summed).astype(BF16)

    load["bc"].wait()
    load["wbc"].wait()
    own_bc[...] = convolve(bc_ref[...], hist_bc[...], wbc_ref)

    bc_copy = pltpu.make_async_remote_copy(
        src_ref=own_bc,
        dst_ref=other_bc,
        send_sem=t_send.at[0],
        recv_sem=t_recv.at[0],
        device_id={"tensor": mate},
        device_id_type=MESH,
    )
    bc_copy.start()

    source = [jnp.int32(-1)] * IN_CAP
    arrived = jnp.int32(0)
    for d in range(n_dp):
        rank = jnp.int32(0)
        for q in range(requests):
            to = dst_ref[d * requests + q]
            mine = to == me
            for k in range(IN_CAP):
                source[k] = jnp.where(mine & (arrived == k), d * MOVE + rank, source[k])
            arrived = arrived + jnp.where(mine, 1, 0)
            rank = rank + jnp.where(to >= 0, 1, 0)

    load["acc"].wait()
    for name in ("hx", "x", "wx", "dt", "bias", "rate"):
        load[name].wait()
    for t in range(3):
        hist_x[8 * t : 8 * t + requests, :] = hx_ref[t].astype(F32)
    x_act = convolve(x_ref[...], hist_x[...], wx_ref)

    head_eye = iota((heads, heads), 0) == iota((heads, heads), 1)

    def head_column(ref):
        return jnp.sum(jnp.where(head_eye, ref[...], 0.0), axis=1, keepdims=True)

    raw = dt_ref[...].astype(F32) + head_column(bias_ref)
    step_t = jnp.maximum(raw, 0.0) + jnp.log1p(jnp.exp(-jnp.abs(raw)))
    step = step_t.T
    log = mm_exact(path, (-head_column(rate_ref) * step_t).T)

    target = jnp.zeros((rows, rows), jnp.int32)
    for r in range(requests):
        target = jnp.where(row // NODES == r, NODES * r + acc_ref[r], target)
    accept_hot = jnp.where(col == target, 1.0, 0.0)
    accept_log = mm_exact(accept_hot, log)
    accept_path = jnp.sum(accept_hot * path.T, axis=1, keepdims=True) > 0.5
    reach = jnp.where(accept_path, accept_log - log, -1e30)
    coef = (jnp.where(accept_path, jnp.exp(reach), 0.0) * step).astype(BF16).astype(F32)
    accept_exp = jnp.exp(accept_log)

    lane_low = iota((1, 2 * P_SIZE), 1) < P_SIZE

    def expand(v):
        return jnp.concatenate(
            [
                jnp.where(lane_low, v[:, 2 * q : 2 * q + 1], v[:, 2 * q + 1 : 2 * q + 2])
                for q in range(heads // 2)
            ],
            axis=1,
        )

    x_float = x_act.astype(F32)
    scaled = expand(coef) * x_float
    scaled_t = scaled.T.astype(BF16)
    xs_rows[...] = scaled.astype(BF16).reshape(xs_rows.shape)

    def tap_rows():
        pick = iota((8 * requests, rows), 0)
        ids = stay + move
        wanted = jnp.zeros((8 * requests, rows), jnp.int32)
        for k in range(requests):
            wanted = jnp.where(pick // 8 == k, NODES * ids[k] + acc_ref[ids[k]], wanted)
        hot = jnp.where(iota((8 * requests, rows), 1) == wanted, 1.0, 0.0)
        turn = pick % 8
        node_part = jnp.where(
            turn == 2, hot, jnp.where(turn == 1, mm(hot, hops[1]), mm(hot, hops[2]))
        )
        turn = iota((8 * requests, hist_rows), 0) % 8
        lag_part = jnp.where(
            turn == 2, 0.0, jnp.where(turn == 1, mm(hot, lags[1]), mm(hot, lags[2]))
        )
        fx = mm(node_part, x_ref[...]) + mm(lag_part, hist_x[...])
        fbc = mm(node_part, bc_ref[...]) + mm(lag_part, hist_bc[...])
        return fx.astype(BF16), fbc.astype(BF16)

    fresh_x, fresh_bc = tap_rows()
    bufs[TAPS][me] = jnp.concatenate([fresh_x[8 * stays :], fresh_bc[8 * stays :]], axis=1)
    for k in range(stays):
        ncx_ref[k] = fresh_x[8 * k : 8 * k + 3]
        ncbc_ref[k] = fresh_bc[8 * k : 8 * k + 3]

    send(TAPS)
    bc_copy.wait()
    own = own_bc[...]
    other = other_bc[...]
    even = (parity == 0).astype(F32)
    own_f = own.astype(F32)
    other_f = other.astype(F32)
    b_act = (even * own_f + (1.0 - even) * other_f).astype(BF16)
    c_act = (even * other_f + (1.0 - even) * own_f).astype(BF16)

    row_request = iota((rows, 1), 0) // NODES
    first_row = iota((rows, 1), 0)
    b_rows[...] = b_act.reshape(b_rows.shape)

    def scale_of(request):
        return jnp.sum(
            jnp.where(first_row == NODES * request, accept_exp, 0.0), axis=0, keepdims=True
        )

    def fresh_of(request):
        b_mine = jnp.where(row_request == request, b_act.astype(F32), 0.0).astype(BF16)
        scale = scale_of(request)

        def chunk(c):
            update = mm(scaled_t[c * depth_rows : (c + 1) * depth_rows], b_mine)
            parts = []
            for h in range(per):
                head = c * per + h
                held = ssm_ref[request, head].astype(F32) * scale[:, head : head + 1]
                parts.append(held + update[h * P_SIZE : (h + 1) * P_SIZE])
            return jnp.concatenate(parts, axis=0).astype(BF16)

        return chunk

    def place(c):
        for j in range(chips):
            beside(c, j, behind(j, 1 - core)).wait_recv()
        for k in range(IN_CAP):
            index = jnp.maximum(source[k], 0)
            there = source[k] >= 0
            if c == TAPS:
                found = bufs[TAPS][index // MOVE].astype(F32)
                found = jnp.where(index % MOVE == 0, found[0:8], found[8:16])
                found = jnp.where(there, found, 0.0).astype(BF16)
                ncx_ref[stays + k] = found[0:3, :width]
                ncbc_ref[stays + k] = found[0:3, width:]
            else:
                found = jnp.where(there, bufs[c][index].astype(F32), 0.0).astype(BF16)
                new_ref[stays + k, c * per : (c + 1) * per] = found.reshape(per, P_SIZE, N)

    raw_width = RAW * depth_rows
    bufs[SCALE][me] = jnp.zeros(bufs[SCALE].shape[1:], F32)
    for k in range(MOVE):
        bufs[SCALE][me, k : k + 1, :heads] = scale_of(move[k])
        bufs[AUX][me * MOVE + k, :, :raw_width] = xs_rows[move[k]][:, :raw_width]
        bufs[AUX][me * MOVE + k, :, raw_width:] = b_rows[move[k]]
    send(SCALE)
    send(AUX)

    def settle(messages):
        for c in messages:
            for j in range(chips):
                beside(c, j, behind(j, 1 - core)).wait_recv()

    def place_raw():
        settle((SCALE, AUX) + tuple(range(RAW)))
        for k in range(IN_CAP):
            index = jnp.maximum(source[k], 0)
            there = source[k] >= 0
            scales = bufs[SCALE][index // MOVE]
            scale = jnp.where(index % MOVE == 0, scales[0:1], scales[1:2])
            both = bufs[AUX][index].astype(F32)
            update = mm(both[:, :raw_width].T, both[:, raw_width:])
            for head in range(RAW * per):
                low = (head % per) * P_SIZE
                held = bufs[head // per][index][low : low + P_SIZE].astype(F32)
                found = held * scale[:, head : head + 1]
                found = found + update[head * P_SIZE : (head + 1) * P_SIZE]
                new_ref[stays + k, head] = jnp.where(there, found, 0.0).astype(BF16)

    movers = [fresh_of(move[k]) for k in range(MOVE)]
    for c in range(RAW, CHUNKS):
        for k in range(MOVE):
            bufs[c][me * MOVE + k] = movers[k](c)
        send(c)
    for c in range(RAW):
        relay(c)

    for name in ("gate", "skip", "gain"):
        load[name].wait()
    inner = lax.dot_general(
        c_act, b_act, (((1,), (1,)), ((), ())), preferred_element_type=F32
    )
    inside = path > 0.5
    inner = jnp.where(inside, inner, 0.0)
    log_t = log.T
    log_exp = expand(jnp.exp(log))
    held = jnp.concatenate(
        [
            lax.dot_general(
                c_act[NODES * r : NODES * (r + 1)],
                ssm_ref[r].reshape(width, N),
                (((1,), (1,)), ((), ())),
                preferred_element_type=F32,
            )
            for r in range(requests)
        ],
        axis=0,
    )
    tree = []
    for q in range(heads // 2):
        pair = x_act[:, 2 * P_SIZE * q : 2 * P_SIZE * (q + 1)]
        both = []
        for h in (2 * q, 2 * q + 1):
            spread = jnp.where(inside, log[:, h : h + 1] - log_t[h : h + 1, :], -1e30)
            weight = inner * jnp.exp(spread) * step_t[h : h + 1, :]
            both.append(mm(weight, pair))
        tree.append(jnp.where(lane_low, both[0], both[1]))
    tree = jnp.concatenate(tree, axis=1)
    mixed = tree + held * log_exp + expand(skip_ref[...]) * x_float
    gated = mixed * silu(gate_ref[...].astype(F32))
    squares = jnp.sum(gated * gated, axis=1, keepdims=True)
    sq_own[...] = jnp.broadcast_to(
        jnp.sum(jnp.where(row == col, squares, 0.0), axis=0, keepdims=True), sq_own.shape
    )
    sq_copy = pltpu.make_async_remote_copy(
        src_ref=sq_own,
        dst_ref=sq_other,
        send_sem=t_send.at[1],
        recv_sem=t_recv.at[1],
        device_id={"tensor": mate},
        device_id_type=MESH,
    )
    sq_copy.start()

    relay(TAPS)
    relay(SCALE)
    relay(AUX)
    for k in range(stays):
        chunk = fresh_of(stay[k])
        for c in range(CHUNKS):
            new_ref[k, c * per : (c + 1) * per] = chunk(c).reshape(per, P_SIZE, N)

    sq_copy.wait()
    partner = jnp.sum(jnp.where(row == col, sq_other[0:1, :], 0.0), axis=1, keepdims=True)
    mean_square = (squares + partner) * (1.0 / (2 * heads * P_SIZE))
    y_ref[...] = (gated * lax.rsqrt(mean_square + 1e-05) * gain_ref[...]).astype(BF16)

    relay(RAW)
    place_raw()
    place(TAPS)
    for c in range(RAW + 1, CHUNKS):
        relay(c)
        place(c - 1)
    place(CHUNKS - 1)
    for c in range(MESSAGES):
        for j in range(1, chips):
            across(c, j, me).wait_send()
        for j in range(chips):
            beside(c, j, behind(j, core)).wait_send()


def write_out(*refs):
    copies = [pltpu.make_async_copy(refs[i], refs[4 + i], refs[8].at[i]) for i in range(4)]
    for copy in copies:
        copy.start()
    for copy in copies:
        copy.wait()


def body(
    x_stream,
    bc_stream,
    gate_stream,
    dt_stream,
    conv_x_state,
    conv_bc_state,
    ssm_state,
    conv_x_weight,
    conv_bc_weight,
    dt_bias,
    decay_rate,
    skip_gain,
    norm_gain,
    parents,
    accepted,
    destination,
):
    n_dp = lax.axis_size("dp")
    chips = n_dp // 2
    rows, width = x_stream.shape
    bc_width = bc_stream.shape[1]
    requests = parents.shape[0]
    heads = dt_stream.shape[1]
    operands = (
        x_stream,
        bc_stream,
        gate_stream,
        dt_stream.T,
        conv_x_state.transpose(1, 0, 2),
        conv_bc_state.transpose(1, 0, 2),
        ssm_state,
        conv_x_weight,
        conv_bc_weight,
        dt_bias.reshape(1, heads),
        decay_rate.reshape(1, heads),
        skip_gain.reshape(1, heads),
        norm_gain.reshape(1, width),
        parents,
        accepted,
        destination,
    )
    vmem = pl.BlockSpec(memory_space=pltpu.VMEM)
    hbm = pl.BlockSpec(memory_space=pltpu.HBM)
    outs = (
        jax.ShapeDtypeStruct((rows, width), BF16),
        jax.ShapeDtypeStruct((KEEP, heads, P_SIZE, N), BF16),
        jax.ShapeDtypeStruct((KEEP, 3, width), BF16),
        jax.ShapeDtypeStruct((KEEP, 3, bc_width), BF16),
    )
    copies = (MESSAGES, chips)
    part = heads // CHUNKS * P_SIZE
    results = pl.pallas_call(
        functools.partial(kernel, n_dp),
        out_shape=outs,
        in_specs=[hbm] * 16,
        out_specs=(vmem,) * 4,
        scratch_shapes=[
            (pltpu.VMEM if i < 14 else pltpu.SMEM)(a.shape, a.dtype)
            for i, a in enumerate(operands)
        ]
        + [
            pltpu.VMEM((32, width), F32),
            pltpu.VMEM((32, bc_width), F32),
            pltpu.VMEM((rows, bc_width), BF16),
            pltpu.VMEM((rows, bc_width), BF16),
            pltpu.VMEM((8, rows), F32),
            pltpu.VMEM((8, rows), F32),
            pltpu.VMEM((requests, NODES, width), BF16),
            pltpu.VMEM((requests, NODES, bc_width), BF16),
        ]
        + [pltpu.VMEM((n_dp * MOVE, part, N), BF16)] * CHUNKS
        + [
            pltpu.VMEM((n_dp, 8 * MOVE, width + bc_width), BF16),
            pltpu.VMEM((n_dp * MOVE, NODES, RAW * part + bc_width), BF16),
            pltpu.VMEM((n_dp, 8, 128), F32),
        ]
        + [pltpu.SemaphoreType.DMA((16,))]
        + [pltpu.SemaphoreType.DMA((2,))] * 2
        + [pltpu.SemaphoreType.DMA(copies)] * 4,
        compiler_params=pltpu.CompilerParams(
            collective_id=0, has_side_effects=True, vmem_limit_bytes=40 << 20
        ),
        name="verify_and_migrate",
    )(*[pltpu.with_memory_space_constraint(a, pltpu.HBM) for a in operands])
    return pl.pallas_call(
        write_out,
        out_shape=outs,
        in_specs=[vmem] * 4,
        out_specs=(hbm,) * 4,
        scratch_shapes=[pltpu.SemaphoreType.DMA((4,))],
        compiler_params=pltpu.CompilerParams(vmem_limit_bytes=16 << 20),
        name="write_out",
    )(*results)


def solution(mesh):
    placed = (
        P(("groups", "dp"), "tensor"),
        P(("groups", "dp"), "tensor"),
        P(("groups", "dp"), "tensor"),
        P(("groups", "dp"), "tensor"),
        P(("groups", "dp"), None, "tensor"),
        P(("groups", "dp"), None, "tensor"),
        P(("groups", "dp"), "tensor", None, None),
        P(None, "tensor"),
        P(None, "tensor"),
        P("tensor"),
        P("tensor"),
        P("tensor"),
        P("tensor"),
        P(("groups", "dp"), None),
        P(("groups", "dp")),
        P("groups"),
    )
    return jax.shard_map(
        body,
        mesh=mesh,
        in_specs=placed,
        out_specs=(
            P(("groups", "dp"), "tensor"),
            P(("groups", "dp"), "tensor", None, None),
            P(("groups", "dp"), None, "tensor"),
            P(("groups", "dp"), None, "tensor"),
        ),
        check_vma=False,
    )
```

```python
import functools

import jax
import jax.numpy as jnp
from jax import lax
from jax.experimental import pallas as pl
from jax.experimental.pallas import tpu as pltpu
from jax.sharding import PartitionSpec as P

P_SIZE = 64
N = 256
NODES = 32
MOVE = 2
IN_CAP = 4
KEEP = 6
CHUNKS = 4
RAW = 2
TAPS, AUX, SCALE = CHUNKS, CHUNKS + 1, CHUNKS + 2
MESSAGES = CHUNKS + 3
MESH = pl.DeviceIdType.MESH
F32 = jnp.float32
BF16 = jnp.bfloat16


def mm(a, b):
    return jnp.dot(a.astype(BF16), b.astype(BF16), preferred_element_type=F32)


def mm_exact(a, b):
    return jnp.dot(a, b, preferred_element_type=F32, precision=lax.Precision.HIGHEST)


def iota(shape, dim):
    return lax.broadcasted_iota(jnp.int32, shape, dim)


def silu(v):
    return v / (1.0 + jnp.exp(-v))


def kernel(n_dp, *refs):
    operands = refs[:16]
    y_ref, new_ref, ncx_ref, ncbc_ref = refs[16:20]
    held_refs = refs[20:36]
    hist_x, hist_bc, own_bc, other_bc, sq_own, sq_other, xs_rows, b_rows = refs[36:44]
    bufs = refs[44 : 44 + MESSAGES]
    in_sem, t_send, t_recv, x_send, x_recv, p_send, p_recv = refs[44 + MESSAGES :]
    (
        x_ref,
        bc_ref,
        gate_ref,
        dt_ref,
        hx_ref,
        hbc_ref,
        ssm_ref,
        wx_ref,
        wbc_ref,
        bias_ref,
        rate_ref,
        skip_ref,
        gain_ref,
        par_ref,
        acc_ref,
        dst_ref,
    ) = held_refs
    loads = [
        pltpu.make_async_copy(operands[i], held_refs[i], in_sem.at[i]) for i in range(16)
    ]
    names = ("x", "bc", "gate", "dt", "hx", "hbc", "ssm", "wx", "wbc")
    names += ("bias", "rate", "skip", "gain", "par", "acc", "dst")
    load = dict(zip(names, loads))
    chips = n_dp // 2
    me = lax.axis_index("dp")
    chip = me // 2
    core = me % 2
    tensor = lax.axis_index("tensor")
    parity = tensor % 2
    mate = tensor + 1 - 2 * parity
    twin = me + 1 - 2 * core

    def ahead(j):
        return 2 * ((chip + j) % chips) + core

    def behind(j, which):
        return 2 * ((chip + chips - j) % chips) + which

    barrier = pltpu.get_barrier_semaphore()
    pl.semaphore_signal(barrier, inc=1, device_id={"tensor": mate}, device_id_type=MESH)
    pl.semaphore_signal(barrier, inc=1, device_id={"dp": twin}, device_id_type=MESH)
    for j in range(1, chips):
        pl.semaphore_signal(barrier, inc=1, device_id={"dp": ahead(j)}, device_id_type=MESH)

    order = ("dst", "ssm", "par", "bc", "hbc", "wbc", "acc", "x", "hx", "wx")
    order += ("dt", "bias", "rate", "gate", "skip", "gain")
    for name in order:
        load[name].start()

    requests = par_ref.shape[0]
    rows = x_ref.shape[0]
    heads = dt_ref.shape[0]
    width = x_ref.shape[1]

    load["dst"].wait()
    stay = [jnp.int32(0)] * (requests - MOVE)
    move = [jnp.int32(0)] * MOVE
    stay_count = jnp.int32(0)
    move_count = jnp.int32(0)
    for q in range(requests):
        staying = dst_ref[me * requests + q] < 0
        for k in range(requests - MOVE):
            stay[k] = jnp.where(staying & (stay_count == k), q, stay[k])
        for k in range(MOVE):
            move[k] = jnp.where(jnp.logical_not(staying) & (move_count == k), q, move[k])
        stay_count = stay_count + jnp.where(staying, 1, 0)
        move_count = move_count + jnp.where(staying, 0, 1)
    stays = requests - MOVE
    per = heads // CHUNKS
    depth_rows = per * P_SIZE

    def block_of(c, device):
        if c in (TAPS, SCALE):
            return bufs[c].at[device]
        return bufs[c].at[pl.ds(device * MOVE, MOVE)]

    def across(c, j, device):
        return pltpu.make_async_remote_copy(
            src_ref=block_of(c, device),
            dst_ref=block_of(c, device),
            send_sem=x_send.at[c, j],
            recv_sem=x_recv.at[c, j],
            device_id={"dp": ahead(j)},
            device_id_type=MESH,
        )

    def beside(c, j, device):
        return pltpu.make_async_remote_copy(
            src_ref=block_of(c, device),
            dst_ref=block_of(c, device),
            send_sem=p_send.at[c, j],
            recv_sem=p_recv.at[c, j],
            device_id={"dp": twin},
            device_id_type=MESH,
        )

    def send(c):
        for j in range(1, chips):
            across(c, j, me).start()
        beside(c, 0, me).start()

    def relay(c):
        for j in range(1, chips):
            across(c, j, behind(j, core)).wait_recv()
            beside(c, j, behind(j, core)).start()

    load["ssm"].wait()
    for c in range(RAW):
        for k in range(MOVE):
            part = ssm_ref[move[k], c * per : (c + 1) * per]
            bufs[c][me * MOVE + k] = part.reshape(depth_rows, N)
    pl.semaphore_wait(barrier, 1 + chips)
    for c in range(RAW):
        send(c)

    load["par"].wait()
    row = iota((rows, rows), 0)
    col = iota((rows, rows), 1)
    tile = (iota((NODES, rows), 1) % NODES == iota((NODES, rows), 0)).astype(F32)
    tiled = mm(par_ref[...].astype(F32), tile)
    owner = iota((requests, rows), 0)
    flat = jnp.where(tiled < -0.5, -1.0, tiled + (NODES * owner).astype(F32))
    flat = jnp.sum(
        jnp.where(iota((requests, rows), 1) // NODES == owner, flat, 0.0), axis=0, keepdims=True
    )
    hop_t = jnp.where(row.astype(F32) == flat, 1.0, 0.0)
    eye = jnp.where(row == col, 1.0, 0.0)
    hop1 = hop_t.T
    hop2 = mm(hop1, hop1)
    hop3 = mm(hop2, hop1)
    hop4 = mm(hop2, hop2)
    hop8 = mm(hop4, hop4)
    hop16 = mm(hop8, hop8)
    path = eye + hop1
    path = path + mm(hop2, path)
    path = path + mm(hop4, path)
    path = path + mm(hop8, path)
    path = path + mm(hop16, path)
    depth = jnp.sum(path, axis=1, keepdims=True) - 1.0
    hops = [eye, hop1, hop2, hop3]
    hist_rows = 32
    hist_row = iota((rows, hist_rows), 1)
    hist_mine = (hist_row % 8 == iota((rows, hist_rows), 0) // NODES) & (hist_row < 24)
    lags = [
        jnp.where(hist_mine & ((hist_row // 8).astype(F32) == 3.0 - k + depth), 1.0, 0.0)
        for k in range(4)
    ]

    hist_x[...] = jnp.zeros(hist_x.shape, F32)
    hist_bc[...] = jnp.zeros(hist_bc.shape, F32)
    load["hbc"].wait()
    for t in range(3):
        hist_bc[8 * t : 8 * t + requests, :] = hbc_ref[t].astype(F32)

    def convolve(values, history, w_ref):
        summed = w_ref[0:1, :].astype(F32) * values.astype(F32)
        for k in range(1, 4):
            tap = mm(hops[k], values) + mm(lags[k], history)
            summed = summed + w_ref[k : k + 1, :].astype(F32) * tap
        return silu(summed).astype(BF16)

    load["bc"].wait()
    load["wbc"].wait()
    own_bc[...] = convolve(bc_ref[...], hist_bc[...], wbc_ref)

    bc_copy = pltpu.make_async_remote_copy(
        src_ref=own_bc,
        dst_ref=other_bc,
        send_sem=t_send.at[0],
        recv_sem=t_recv.at[0],
        device_id={"tensor": mate},
        device_id_type=MESH,
    )
    bc_copy.start()

    source = [jnp.int32(-1)] * IN_CAP
    arrived = jnp.int32(0)
    for d in range(n_dp):
        rank = jnp.int32(0)
        for q in range(requests):
            to = dst_ref[d * requests + q]
            mine = to == me
            for k in range(IN_CAP):
                source[k] = jnp.where(mine & (arrived == k), d * MOVE + rank, source[k])
            arrived = arrived + jnp.where(mine, 1, 0)
            rank = rank + jnp.where(to >= 0, 1, 0)

    load["acc"].wait()
    for name in ("hx", "x", "wx", "dt", "bias", "rate"):
        load[name].wait()
    for t in range(3):
        hist_x[8 * t : 8 * t + requests, :] = hx_ref[t].astype(F32)
    x_act = convolve(x_ref[...], hist_x[...], wx_ref)

    head_eye = iota((heads, heads), 0) == iota((heads, heads), 1)

    def head_column(ref):
        return jnp.sum(jnp.where(head_eye, ref[...], 0.0), axis=1, keepdims=True)

    raw = dt_ref[...].astype(F32) + head_column(bias_ref)
    step_t = jnp.maximum(raw, 0.0) + jnp.log1p(jnp.exp(-jnp.abs(raw)))
    step = step_t.T
    log = mm_exact(path, (-head_column(rate_ref) * step_t).T)

    target = jnp.zeros((rows, rows), jnp.int32)
    for r in range(requests):
        target = jnp.where(row // NODES == r, NODES * r + acc_ref[r], target)
    accept_hot = jnp.where(col == target, 1.0, 0.0)
    accept_log = mm_exact(accept_hot, log)
    accept_path = jnp.sum(accept_hot * path.T, axis=1, keepdims=True) > 0.5
    reach = jnp.where(accept_path, accept_log - log, -1e30)
    coef = (jnp.where(accept_path, jnp.exp(reach), 0.0) * step).astype(BF16).astype(F32)
    accept_exp = jnp.exp(accept_log)

    lane_low = iota((1, 2 * P_SIZE), 1) < P_SIZE

    def expand(v):
        return jnp.concatenate(
            [
                jnp.where(lane_low, v[:, 2 * q : 2 * q + 1], v[:, 2 * q + 1 : 2 * q + 2])
                for q in range(heads // 2)
            ],
            axis=1,
        )

    x_float = x_act.astype(F32)
    scaled = expand(coef) * x_float
    scaled_t = scaled.T.astype(BF16)
    xs_rows[...] = scaled.astype(BF16).reshape(xs_rows.shape)

    def tap_rows():
        pick = iota((8 * requests, rows), 0)
        ids = stay + move
        wanted = jnp.zeros((8 * requests, rows), jnp.int32)
        for k in range(requests):
            wanted = jnp.where(pick // 8 == k, NODES * ids[k] + acc_ref[ids[k]], wanted)
        hot = jnp.where(iota((8 * requests, rows), 1) == wanted, 1.0, 0.0)
        turn = pick % 8
        node_part = jnp.where(
            turn == 2, hot, jnp.where(turn == 1, mm(hot, hops[1]), mm(hot, hops[2]))
        )
        turn = iota((8 * requests, hist_rows), 0) % 8
        lag_part = jnp.where(
            turn == 2, 0.0, jnp.where(turn == 1, mm(hot, lags[1]), mm(hot, lags[2]))
        )
        fx = mm(node_part, x_ref[...]) + mm(lag_part, hist_x[...])
        fbc = mm(node_part, bc_ref[...]) + mm(lag_part, hist_bc[...])
        return fx.astype(BF16), fbc.astype(BF16)

    fresh_x, fresh_bc = tap_rows()
    bufs[TAPS][me] = jnp.concatenate([fresh_x[8 * stays :], fresh_bc[8 * stays :]], axis=1)
    for k in range(stays):
        ncx_ref[k] = fresh_x[8 * k : 8 * k + 3]
        ncbc_ref[k] = fresh_bc[8 * k : 8 * k + 3]

    send(TAPS)
    bc_copy.wait()
    for c in range(RAW):
        relay(c)
    own = own_bc[...]
    other = other_bc[...]
    even = (parity == 0).astype(F32)
    own_f = own.astype(F32)
    other_f = other.astype(F32)
    b_act = (even * own_f + (1.0 - even) * other_f).astype(BF16)
    c_act = (even * other_f + (1.0 - even) * own_f).astype(BF16)

    row_request = iota((rows, 1), 0) // NODES
    first_row = iota((rows, 1), 0)
    b_rows[...] = b_act.reshape(b_rows.shape)

    def scale_of(request):
        return jnp.sum(
            jnp.where(first_row == NODES * request, accept_exp, 0.0), axis=0, keepdims=True
        )

    def fresh_of(request):
        b_mine = jnp.where(row_request == request, b_act.astype(F32), 0.0).astype(BF16)
        scale = scale_of(request)

        def chunk(c):
            update = mm(scaled_t[c * depth_rows : (c + 1) * depth_rows], b_mine)
            parts = []
            for h in range(per):
                head = c * per + h
                held = ssm_ref[request, head].astype(F32) * scale[:, head : head + 1]
                parts.append(held + update[h * P_SIZE : (h + 1) * P_SIZE])
            return jnp.concatenate(parts, axis=0).astype(BF16)

        return chunk

    def place(c):
        for j in range(chips):
            beside(c, j, behind(j, 1 - core)).wait_recv()
        for k in range(IN_CAP):
            index = jnp.maximum(source[k], 0)
            there = source[k] >= 0
            if c == TAPS:
                found = bufs[TAPS][index // MOVE].astype(F32)
                found = jnp.where(index % MOVE == 0, found[0:8], found[8:16])
                found = jnp.where(there, found, 0.0).astype(BF16)
                ncx_ref[stays + k] = found[0:3, :width]
                ncbc_ref[stays + k] = found[0:3, width:]
            else:
                found = jnp.where(there, bufs[c][index].astype(F32), 0.0).astype(BF16)
                new_ref[stays + k, c * per : (c + 1) * per] = found.reshape(per, P_SIZE, N)

    raw_width = RAW * depth_rows
    bufs[SCALE][me] = jnp.zeros(bufs[SCALE].shape[1:], F32)
    for k in range(MOVE):
        bufs[SCALE][me, k : k + 1, :heads] = scale_of(move[k])
        bufs[AUX][me * MOVE + k, :, :raw_width] = xs_rows[move[k]][:, :raw_width]
        bufs[AUX][me * MOVE + k, :, raw_width:] = b_rows[move[k]]
    send(SCALE)
    send(AUX)

    def settle(messages):
        for c in messages:
            for j in range(chips):
                beside(c, j, behind(j, 1 - core)).wait_recv()

    def place_raw():
        settle((SCALE, AUX) + tuple(range(RAW)))
        for k in range(IN_CAP):
            index = jnp.maximum(source[k], 0)
            there = source[k] >= 0
            scales = bufs[SCALE][index // MOVE]
            scale = jnp.where(index % MOVE == 0, scales[0:1], scales[1:2])
            both = bufs[AUX][index].astype(F32)
            update = mm(both[:, :raw_width].T, both[:, raw_width:])
            for head in range(RAW * per):
                low = (head % per) * P_SIZE
                held = bufs[head // per][index][low : low + P_SIZE].astype(F32)
                found = held * scale[:, head : head + 1]
                found = found + update[head * P_SIZE : (head + 1) * P_SIZE]
                new_ref[stays + k, head] = jnp.where(there, found, 0.0).astype(BF16)

    movers = [fresh_of(move[k]) for k in range(MOVE)]
    for c in range(RAW, CHUNKS):
        for k in range(MOVE):
            bufs[c][me * MOVE + k] = movers[k](c)
        send(c)
    for name in ("gate", "skip", "gain"):
        load[name].wait()
    inner = lax.dot_general(
        c_act, b_act, (((1,), (1,)), ((), ())), preferred_element_type=F32
    )
    inside = path > 0.5
    inner = jnp.where(inside, inner, 0.0)
    log_t = log.T
    log_exp = expand(jnp.exp(log))
    held = jnp.concatenate(
        [
            lax.dot_general(
                c_act[NODES * r : NODES * (r + 1)],
                ssm_ref[r].reshape(width, N),
                (((1,), (1,)), ((), ())),
                preferred_element_type=F32,
            )
            for r in range(requests)
        ],
        axis=0,
    )
    tree = []
    for q in range(heads // 2):
        pair = x_act[:, 2 * P_SIZE * q : 2 * P_SIZE * (q + 1)]
        both = []
        for h in (2 * q, 2 * q + 1):
            spread = jnp.where(inside, log[:, h : h + 1] - log_t[h : h + 1, :], -1e30)
            weight = inner * jnp.exp(spread) * step_t[h : h + 1, :]
            both.append(mm(weight, pair))
        tree.append(jnp.where(lane_low, both[0], both[1]))
    tree = jnp.concatenate(tree, axis=1)
    mixed = tree + held * log_exp + expand(skip_ref[...]) * x_float
    gated = mixed * silu(gate_ref[...].astype(F32))
    squares = jnp.sum(gated * gated, axis=1, keepdims=True)
    sq_own[...] = jnp.broadcast_to(
        jnp.sum(jnp.where(row == col, squares, 0.0), axis=0, keepdims=True), sq_own.shape
    )
    sq_copy = pltpu.make_async_remote_copy(
        src_ref=sq_own,
        dst_ref=sq_other,
        send_sem=t_send.at[1],
        recv_sem=t_recv.at[1],
        device_id={"tensor": mate},
        device_id_type=MESH,
    )
    sq_copy.start()

    relay(TAPS)
    relay(SCALE)
    relay(AUX)
    for k in range(stays):
        chunk = fresh_of(stay[k])
        for c in range(CHUNKS):
            new_ref[k, c * per : (c + 1) * per] = chunk(c).reshape(per, P_SIZE, N)

    sq_copy.wait()
    partner = jnp.sum(jnp.where(row == col, sq_other[0:1, :], 0.0), axis=1, keepdims=True)
    mean_square = (squares + partner) * (1.0 / (2 * heads * P_SIZE))
    y_ref[...] = (gated * lax.rsqrt(mean_square + 1e-05) * gain_ref[...]).astype(BF16)

    relay(RAW)
    place_raw()
    place(TAPS)
    for c in range(RAW + 1, CHUNKS):
        relay(c)
        place(c - 1)
    place(CHUNKS - 1)
    for c in range(MESSAGES):
        for j in range(1, chips):
            across(c, j, me).wait_send()
        for j in range(chips):
            beside(c, j, behind(j, core)).wait_send()


def write_out(*refs):
    copies = [pltpu.make_async_copy(refs[i], refs[4 + i], refs[8].at[i]) for i in range(4)]
    for copy in copies:
        copy.start()
    for copy in copies:
        copy.wait()


def body(
    x_stream,
    bc_stream,
    gate_stream,
    dt_stream,
    conv_x_state,
    conv_bc_state,
    ssm_state,
    conv_x_weight,
    conv_bc_weight,
    dt_bias,
    decay_rate,
    skip_gain,
    norm_gain,
    parents,
    accepted,
    destination,
):
    n_dp = lax.axis_size("dp")
    chips = n_dp // 2
    rows, width = x_stream.shape
    bc_width = bc_stream.shape[1]
    requests = parents.shape[0]
    heads = dt_stream.shape[1]
    operands = (
        x_stream,
        bc_stream,
        gate_stream,
        dt_stream.T,
        conv_x_state.transpose(1, 0, 2),
        conv_bc_state.transpose(1, 0, 2),
        ssm_state,
        conv_x_weight,
        conv_bc_weight,
        dt_bias.reshape(1, heads),
        decay_rate.reshape(1, heads),
        skip_gain.reshape(1, heads),
        norm_gain.reshape(1, width),
        parents,
        accepted,
        destination,
    )
    vmem = pl.BlockSpec(memory_space=pltpu.VMEM)
    hbm = pl.BlockSpec(memory_space=pltpu.HBM)
    outs = (
        jax.ShapeDtypeStruct((rows, width), BF16),
        jax.ShapeDtypeStruct((KEEP, heads, P_SIZE, N), BF16),
        jax.ShapeDtypeStruct((KEEP, 3, width), BF16),
        jax.ShapeDtypeStruct((KEEP, 3, bc_width), BF16),
    )
    copies = (MESSAGES, chips)
    part = heads // CHUNKS * P_SIZE
    results = pl.pallas_call(
        functools.partial(kernel, n_dp),
        out_shape=outs,
        in_specs=[hbm] * 16,
        out_specs=(vmem,) * 4,
        scratch_shapes=[
            (pltpu.VMEM if i < 14 else pltpu.SMEM)(a.shape, a.dtype)
            for i, a in enumerate(operands)
        ]
        + [
            pltpu.VMEM((32, width), F32),
            pltpu.VMEM((32, bc_width), F32),
            pltpu.VMEM((rows, bc_width), BF16),
            pltpu.VMEM((rows, bc_width), BF16),
            pltpu.VMEM((8, rows), F32),
            pltpu.VMEM((8, rows), F32),
            pltpu.VMEM((requests, NODES, width), BF16),
            pltpu.VMEM((requests, NODES, bc_width), BF16),
        ]
        + [pltpu.VMEM((n_dp * MOVE, part, N), BF16)] * CHUNKS
        + [
            pltpu.VMEM((n_dp, 8 * MOVE, width + bc_width), BF16),
            pltpu.VMEM((n_dp * MOVE, NODES, RAW * part + bc_width), BF16),
            pltpu.VMEM((n_dp, 8, 128), F32),
        ]
        + [pltpu.SemaphoreType.DMA((16,))]
        + [pltpu.SemaphoreType.DMA((2,))] * 2
        + [pltpu.SemaphoreType.DMA(copies)] * 4,
        compiler_params=pltpu.CompilerParams(
            collective_id=0, has_side_effects=True, vmem_limit_bytes=40 << 20
        ),
        name="verify_and_migrate",
    )(*[pltpu.with_memory_space_constraint(a, pltpu.HBM) for a in operands])
    return pl.pallas_call(
        write_out,
        out_shape=outs,
        in_specs=[vmem] * 4,
        out_specs=(hbm,) * 4,
        scratch_shapes=[pltpu.SemaphoreType.DMA((4,))],
        compiler_params=pltpu.CompilerParams(vmem_limit_bytes=16 << 20),
        name="write_out",
    )(*results)


def solution(mesh):
    placed = (
        P(("groups", "dp"), "tensor"),
        P(("groups", "dp"), "tensor"),
        P(("groups", "dp"), "tensor"),
        P(("groups", "dp"), "tensor"),
        P(("groups", "dp"), None, "tensor"),
        P(("groups", "dp"), None, "tensor"),
        P(("groups", "dp"), "tensor", None, None),
        P(None, "tensor"),
        P(None, "tensor"),
        P("tensor"),
        P("tensor"),
        P("tensor"),
        P("tensor"),
        P(("groups", "dp"), None),
        P(("groups", "dp")),
        P("groups"),
    )
    return jax.shard_map(
        body,
        mesh=mesh,
        in_specs=placed,
        out_specs=(
            P(("groups", "dp"), "tensor"),
            P(("groups", "dp"), "tensor", None, None),
            P(("groups", "dp"), None, "tensor"),
            P(("groups", "dp"), None, "tensor"),
        ),
        check_vma=False,
    )
```
